32 devices in a mesh: groups: 2 (over y), fsdp: 4 (over z), owner: 4 (over x, core).
Axes of the slice: x: 2, y: 2, z: 4, core: 2. Of those that a mesh axis runs over, the one named last changes fastest.
Arguments:
- inputs: bfloat16 [13312, 8192], P(('groups', 'fsdp'), 'owner'), parts along dimension 0, may hold values from -6 to 6
- value_matrix: bfloat16 [1024, 8192], P('fsdp', 'owner'), may hold values from -0.0625 to 0.0625
- adapter_down_weight: float32 [8, 64, 8192], P(('groups', 'fsdp'), None, 'owner'), parts along dimension 0, may hold values from -6 to 6
- adapter_up_weight: float32 [8, 64, 1024], P(('groups', 'fsdp'), None, 'owner'), parts along dimension 0, may hold values from -6 to 6
- down_first_moment: float32 [8, 64, 8192], P(('groups', 'fsdp'), None, 'owner'), parts along dimension 0, may hold values from -2 to 2
- down_second_moment: float32 [8, 64, 8192], P(('groups', 'fsdp'), None, 'owner'), parts along dimension 0, may hold values from 0.05 to 2
- up_first_moment: float32 [8, 64, 1024], P(('groups', 'fsdp'), None, 'owner'), parts along dimension 0, may hold values from -2 to 2
- up_second_moment: float32 [8, 64, 1024], P(('groups', 'fsdp'), None, 'owner'), parts along dimension 0, may hold values from 0.05 to 2
- output_gradient: bfloat16 [13312, 1024], P(('groups', 'fsdp'), 'owner'), parts along dimension 0, may hold values from -6 to 6
- tenant_of_block: int32 [104], P('groups'), parts along dimension 0, may hold values from 0 to 3, as said below
- tenant_storage_slot: int32 [8], P('groups'), parts along dimension 0, may hold values from 0 to 3, as said below
Outputs:
- values: bfloat16 [13312, 1024], P(('groups', 'fsdp'), 'owner'), parts along dimension 0
- updated_down_weight: float32 [8, 64, 8192], P(('groups', 'fsdp'), None, 'owner'), parts along dimension 0
- updated_up_weight: float32 [8, 64, 1024], P(('groups', 'fsdp'), None, 'owner'), parts along dimension 0
- updated_down_first: float32 [8, 64, 8192], P(('groups', 'fsdp'), None, 'owner'), parts along dimension 0
- updated_down_second: float32 [8, 64, 8192], P(('groups', 'fsdp'), None, 'owner'), parts along dimension 0
- updated_up_first: float32 [8, 64, 1024], P(('groups', 'fsdp'), None, 'owner'), parts along dimension 0
- updated_up_second: float32 [8, 64, 1024], P(('groups', 'fsdp'), None, 'owner'), parts along dimension 0
The draws below stay inside these ranges and needn't reach their ends.
There are 2 independent parts, one for each index of `groups`. The reference program is written for one: setup_inputs(seed, part) draws one part's arguments, and reference() takes and returns one part's arrays. A program takes and returns all parts, laid end to end along the dimension named above; an argument that names none is the same for every part. Nothing has to cross between parts.
Inputs may be any that keep to these rules, and one draw needn't show every extreme that they name: `tenant_storage_slot`: A permutation of the slots. Slot s is stored on index s of fsdp. `tenant_of_block`: the 13 blocks of one bin use at most one slot stored on each fsdp index; the first min(13, 4) blocks of a bin lie on distinct fsdp indices, and block b + 4 of a bin has the tenant of block b.
All inputs are finite; a program needn't handle non-finite values.
Results may differ from the reference program's by a relative error of at most 0.0045.
Values may be sent and summed in bfloat16 or wider, within the bound.
A program may use at most 128 MiB of HBM per device.

```python
import math
import jax
import jax.numpy as jnp
from jax import lax

MODEL_WIDTH = 8192
VALUE_WIDTH = 1024
ADAPTER_RANK = 64
BLOCK = 128
ADP_DEV = 1
TOK_DEV = 1664
NB = 13
ADAPTER_TOTAL = 4
TOKENS = 6656
N_FSDP = 4


def tenant_plan(key):
    order_key, owner_key, local_key = jax.random.split(key, 3)
    tenant_to_slot = jax.random.permutation(order_key, ADAPTER_TOTAL).astype(jnp.int32)
    bin_keys = jax.random.split(owner_key, N_FSDP)
    orders = jax.vmap(lambda k: jax.random.permutation(k, N_FSDP))(bin_keys).astype(jnp.int32)
    columns = jnp.arange(NB, dtype=jnp.int32) % N_FSDP
    owners = jnp.take(orders, columns, axis=1).astype(jnp.int32)
    local_table = jax.random.randint(local_key, (N_FSDP, N_FSDP), 0, ADP_DEV).astype(jnp.int32)
    local_pick = jnp.take_along_axis(local_table, owners, axis=1)
    slots = owners * ADP_DEV + local_pick
    slot_to_tenant = jnp.zeros((ADAPTER_TOTAL,), jnp.int32).at[tenant_to_slot].set(jnp.arange(ADAPTER_TOTAL, dtype=jnp.int32))
    tenants = jnp.take(slot_to_tenant, slots.reshape(-1), axis=0)
    return (tenant_to_slot, tenants.astype(jnp.int32))


def draw_tenant_storage_slot(key, part):
    return tenant_plan(key)[0]


def draw_tenant_of_block(key, part):
    return tenant_plan(key)[1]


def steps_of(stream_key, dims, cuts, least, high):
    def one(position, blocks):
        steps = jax.random.uniform(jax.random.fold_in(jax.random.fold_in(stream_key, 6), position), (blocks,), jnp.float32, least / len(cuts), high / len(cuts))
        return jnp.repeat(jnp.exp(steps), dims[position] // blocks).reshape((-1,) + (1,) * (len(dims) - position - 1))

    gain = one(*cuts[0])
    for cut in cuts[1:]:
        gain = gain * one(*cut)
    return gain


def noise(own_key, dims, width, reach, cuts=(), kind=jnp.bfloat16):
    gain = steps_of(own_key, dims, cuts, -0.22, 0.18) if cuts else 1.0
    values = jax.random.normal(own_key, dims, jnp.float32) * width * gain
    return jnp.minimum(jnp.maximum(values, -reach), reach).astype(kind)


def setup_inputs(seed: int = 0, part: int = 0) -> dict:
    seeds = jax.random.split(jax.random.key(seed), 12)
    own_keys = jax.random.split(jax.random.fold_in(seeds[11], part), 12)
    inputs = noise(own_keys[0], (TOKENS, MODEL_WIDTH), 1.0, 6.0, ((0, 4), (1, 4)))
    value_matrix = noise(seeds[1], (VALUE_WIDTH, MODEL_WIDTH), MODEL_WIDTH ** -0.5, 0.0625, ((0, 4), (1, 4)))
    adapter_down_weight = noise(own_keys[2], (ADAPTER_TOTAL, ADAPTER_RANK, MODEL_WIDTH), 1.0, 6.0, ((0, 4), (2, 4)), jnp.float32)
    adapter_up_weight = noise(own_keys[3], (ADAPTER_TOTAL, ADAPTER_RANK, VALUE_WIDTH), 1.0, 6.0, ((0, 4), (2, 4)), jnp.float32)
    down_first_moment = noise(own_keys[4], (ADAPTER_TOTAL, ADAPTER_RANK, MODEL_WIDTH), 0.3, 2.0, ((0, 4), (2, 4)), jnp.float32)
    down_second_moment = jnp.clip(jnp.exp(math.log(2.0) - 3.6888794 * jax.random.uniform(own_keys[5], (ADAPTER_TOTAL, ADAPTER_RANK, MODEL_WIDTH), jnp.float32) ** steps_of(own_keys[5], (ADAPTER_TOTAL, ADAPTER_RANK, MODEL_WIDTH), ((0, 4), (2, 4)), -0.2, 0.2)), 0.05, 2.0)
    up_first_moment = noise(own_keys[6], (ADAPTER_TOTAL, ADAPTER_RANK, VALUE_WIDTH), 0.3, 2.0, ((0, 4), (2, 4)), jnp.float32)
    up_second_moment = jnp.clip(jnp.exp(math.log(2.0) - 3.6888794 * jax.random.uniform(own_keys[7], (ADAPTER_TOTAL, ADAPTER_RANK, VALUE_WIDTH), jnp.float32) ** steps_of(own_keys[7], (ADAPTER_TOTAL, ADAPTER_RANK, VALUE_WIDTH), ((0, 4), (2, 4)), -0.2, 0.2)), 0.05, 2.0)
    output_gradient = noise(own_keys[8], (TOKENS, VALUE_WIDTH), 1.0, 6.0, ((0, 4), (1, 4)))
    tenant_of_block = draw_tenant_of_block(jax.random.fold_in(jax.random.fold_in(seeds[11], part), 71), part)
    tenant_storage_slot = draw_tenant_storage_slot(jax.random.fold_in(jax.random.fold_in(seeds[11], part), 71), part)
    return dict(inputs=inputs, value_matrix=value_matrix, adapter_down_weight=adapter_down_weight, adapter_up_weight=adapter_up_weight, down_first_moment=down_first_moment, down_second_moment=down_second_moment, up_first_moment=up_first_moment, up_second_moment=up_second_moment, output_gradient=output_gradient, tenant_of_block=tenant_of_block, tenant_storage_slot=tenant_storage_slot)


branch_scale = 0.5
first_moment = 0.9
second_moment = 0.999
learning_rate = 0.05
decay_rate = 0.01
epsilon = 1e-08
first_correction = 1.0 - math.exp(100.0 * math.log(0.9))
second_correction = 1.0 - math.exp(100.0 * math.log(0.999))

def adam_weight_update(weights, moment, second, gradient):
    new_moment = first_moment * moment + (1.0 - first_moment) * gradient
    new_second = second_moment * second + (1.0 - second_moment) * gradient * gradient
    direction = new_moment / first_correction / (jnp.sqrt(new_second / second_correction) + epsilon)
    new_weights = weights - learning_rate * (direction + decay_rate * weights)
    return (new_weights, new_moment, new_second)

def reference(inputs, value_matrix, adapter_down_weight, adapter_up_weight, down_first_moment, down_second_moment, up_first_moment, up_second_moment, output_gradient, tenant_of_block, tenant_storage_slot):
    highest = lax.Precision.HIGHEST
    tenant_ids = jnp.arange(ADAPTER_TOTAL, dtype=jnp.int32)
    slots = lax.optimization_barrier(jnp.sum(jnp.where(tenant_of_block[:, None] == tenant_ids[None, :], tenant_storage_slot[None, :], 0), axis=1)).astype(jnp.int32)
    down_portion = adapter_down_weight.astype(jnp.bfloat16)
    up_portion = adapter_up_weight.astype(jnp.bfloat16)
    down_factor = 1.0 / math.sqrt(MODEL_WIDTH)
    up_factor = branch_scale / math.sqrt(ADAPTER_RANK)
    row_bins = inputs.reshape(N_FSDP, TOK_DEV, MODEL_WIDTH)
    grad_bins = output_gradient.reshape(N_FSDP, TOK_DEV, VALUE_WIDTH)
    slot_bins = slots.reshape(N_FSDP, NB)

    def one_bin(carry, pieces):
        down_gradient, up_gradient = carry
        rows, cotangent, bin_slots = pieces
        base_values = jnp.dot(rows, value_matrix.T, preferred_element_type=jnp.float32)
        block_down = jnp.take(down_portion, bin_slots, axis=0).astype(jnp.float32)
        block_up = jnp.take(up_portion, bin_slots, axis=0).astype(jnp.float32)
        row_blocks = rows.reshape(NB, BLOCK, MODEL_WIDTH).astype(jnp.float32)
        grad_blocks = cotangent.reshape(NB, BLOCK, VALUE_WIDTH).astype(jnp.float32)
        low = jnp.einsum('btk,brk->brt', row_blocks, block_down, precision=highest) * down_factor
        low_half = low.astype(jnp.bfloat16).astype(jnp.float32)
        extra = jnp.einsum('brt,brj->btj', low_half, block_up, precision=highest) * up_factor
        values = (base_values + extra.reshape(TOK_DEV, VALUE_WIDTH)).astype(jnp.bfloat16)
        back = jnp.einsum('btj,brj->brt', grad_blocks, block_up, precision=highest) * up_factor
        back_half = back.astype(jnp.bfloat16).astype(jnp.float32)
        up_blocks = jnp.einsum('brt,btj->brj', low_half, grad_blocks, precision=highest) * up_factor
        down_blocks = jnp.einsum('brt,btk->brk', back_half, row_blocks, precision=highest) * down_factor
        select = (bin_slots[:, None] == tenant_ids[None, :]).astype(jnp.float32)
        bin_up = jnp.einsum('ba,brj->arj', select, up_blocks, precision=highest).astype(jnp.bfloat16)
        bin_down = jnp.einsum('ba,brk->ark', select, down_blocks, precision=highest).astype(jnp.bfloat16)
        bin_up = lax.optimization_barrier(bin_up)
        bin_down = lax.optimization_barrier(bin_down)
        up_gradient = up_gradient + bin_up.astype(jnp.float32)
        down_gradient = down_gradient + bin_down.astype(jnp.float32)
        return ((down_gradient, up_gradient), values)
    start = (jnp.zeros((ADAPTER_TOTAL, ADAPTER_RANK, MODEL_WIDTH), jnp.float32), jnp.zeros((ADAPTER_TOTAL, ADAPTER_RANK, VALUE_WIDTH), jnp.float32))
    (down_gradient, up_gradient), value_bins = lax.scan(one_bin, start, (row_bins, grad_bins, slot_bins))
    values = value_bins.reshape(TOKENS, VALUE_WIDTH)
    updated_down_weight, updated_down_first, updated_down_second = adam_weight_update(adapter_down_weight, down_first_moment, down_second_moment, down_gradient)
    updated_up_weight, updated_up_first, updated_up_second = adam_weight_update(adapter_up_weight, up_first_moment, up_second_moment, up_gradient)
    return (values, updated_down_weight, updated_up_weight, updated_down_first, updated_down_second, updated_up_first, updated_up_second)
```

```python
import math

import jax
import jax.numpy as jnp
from jax import lax
from jax.experimental import pallas as pl
from jax.experimental.pallas import tpu as pltpu
from jax.sharding import PartitionSpec as P

MODEL_WIDTH = 8192
BLOCK = 128


branch_scale = 0.5
first_moment = 0.9
second_moment = 0.999
learning_rate = 0.05
decay_rate = 0.01
epsilon = 1e-08
first_correction = 1.0 - math.exp(100.0 * math.log(0.9))
second_correction = 1.0 - math.exp(100.0 * math.log(0.999))


def adam_weight_update(weights, moment, second, gradient):
    new_moment = first_moment * moment + (1.0 - first_moment) * gradient
    new_second = second_moment * second + (1.0 - second_moment) * gradient * gradient
    direction = new_moment / first_correction / (jnp.sqrt(new_second / second_correction) + epsilon)
    new_weights = weights - learning_rate * (direction + decay_rate * weights)
    return (new_weights, new_moment, new_second)


def base_product(inputs, value_matrix):
    return jnp.einsum(
        "tk,jk->tj",
        inputs,
        lax.all_gather(value_matrix, "fsdp", axis=0, tiled=True),
        preferred_element_type=jnp.float32,
    )


def finish_values(base_values, low, block_up, up_factor):
    low_half = low.astype(jnp.bfloat16)
    extra = (
        jnp.einsum("brt,brj->btj", low_half, block_up, preferred_element_type=jnp.float32)
        * up_factor
    )
    return (low_half, (base_values + extra.reshape(base_values.shape)).astype(jnp.bfloat16))


def per_device(
    inputs,
    value_matrix,
    adapter_down_weight,
    adapter_up_weight,
    down_first_moment,
    down_second_moment,
    up_first_moment,
    up_second_moment,
    output_gradient,
    tenant_of_block,
    tenant_storage_slot,
):
    highest = lax.Precision.HIGHEST
    bin_count = lax.axis_size("fsdp")
    my_index = lax.axis_index("fsdp")
    tok_rows, quarter = inputs.shape
    block_count = tok_rows // BLOCK
    per_worker_share = adapter_down_weight.shape[0]
    adapter_rank_size = adapter_down_weight.shape[1]
    column_portion = adapter_up_weight.shape[2]
    adapter_count = tenant_storage_slot.shape[0]
    tenant_ids = jnp.arange(adapter_count, dtype=jnp.int32)
    slot_of_block = jnp.sum(
        jnp.where(tenant_of_block[:, None] == tenant_ids[None, :], tenant_storage_slot[None, :], 0),
        axis=1,
    )
    slot_grid = slot_of_block.reshape(bin_count, block_count)
    owner_grid = slot_grid // per_worker_share
    local_grid = slot_grid % per_worker_share
    local_ids = jnp.arange(per_worker_share, dtype=jnp.int32)
    wanted = jnp.any(
        (owner_grid[:, :, None] == my_index) & (local_grid[:, :, None] == local_ids[None, None, :]),
        axis=1,
    )
    chosen = wanted.astype(jnp.bfloat16)
    down_portion = adapter_down_weight.astype(jnp.bfloat16)
    up_portion = adapter_up_weight.astype(jnp.bfloat16)
    my_owners = lax.dynamic_index_in_dim(owner_grid, my_index, 0, keepdims=False)
    partial_value = base_product(inputs, value_matrix)
    send_down = jnp.einsum(
        "fj,jrk->frk", chosen, down_portion, preferred_element_type=jnp.float32
    ).astype(jnp.bfloat16)
    send_up = jnp.einsum(
        "fj,jrk->frk", chosen, up_portion, preferred_element_type=jnp.float32
    ).astype(jnp.bfloat16)
    arrived_down, arrived_up = (
        lax.all_to_all(send_down, "fsdp", split_axis=0, concat_axis=0, tiled=True),
        lax.all_to_all(send_up, "fsdp", split_axis=0, concat_axis=0, tiled=True),
    )
    block_down = jnp.take(arrived_down, my_owners, axis=0)
    block_up = jnp.take(arrived_up, my_owners, axis=0)
    row_blocks = inputs.reshape(block_count, BLOCK, quarter)
    grad_blocks = output_gradient.reshape(block_count, BLOCK, column_portion)
    down_factor = 1.0 / math.sqrt(MODEL_WIDTH)
    up_factor = branch_scale / math.sqrt(adapter_rank_size)
    low_part = (
        jnp.einsum("brk,btk->brt", block_down, row_blocks, preferred_element_type=jnp.float32)
        * down_factor
    )
    back_part = (
        jnp.einsum("btj,brj->brt", grad_blocks, block_up, preferred_element_type=jnp.float32)
        * up_factor
    )
    base_values = lax.psum_scatter(partial_value, "owner", scatter_dimension=1, tiled=True)
    low = lax.psum(low_part, "owner")
    low_half, values = finish_values(base_values, low, block_up, up_factor)
    back = lax.psum(back_part.astype(jnp.bfloat16), "owner")
    up_blocks = (
        jnp.einsum("brt,btj->brj", low_half, grad_blocks, preferred_element_type=jnp.float32)
        * up_factor
    )
    down_blocks = (
        jnp.einsum("brt,btk->brk", back, row_blocks, preferred_element_type=jnp.float32)
        * down_factor
    )
    route = (my_owners[:, None] == jnp.arange(bin_count, dtype=jnp.int32)[None, :]).astype(
        jnp.float32
    )
    back_down = jnp.einsum("bg,brk->grk", route, down_blocks, precision=highest).astype(
        jnp.bfloat16
    )
    back_up = jnp.einsum("bg,brj->grj", route, up_blocks, precision=highest).astype(jnp.bfloat16)
    returned_down, returned_up = (
        lax.all_to_all(back_down, "fsdp", split_axis=0, concat_axis=0, tiled=True),
        lax.all_to_all(back_up, "fsdp", split_axis=0, concat_axis=0, tiled=True),
    )
    down_gradient = jnp.einsum(
        "fj,frk->jrk", chosen, returned_down, preferred_element_type=jnp.float32
    )
    up_gradient = jnp.einsum("fj,frk->jrk", chosen, returned_up, preferred_element_type=jnp.float32)
    updated_down_weight, updated_down_first, updated_down_second = adam_weight_update(
        adapter_down_weight, down_first_moment, down_second_moment, down_gradient
    )
    updated_up_weight, updated_up_first, updated_up_second = adam_weight_update(
        adapter_up_weight, up_first_moment, up_second_moment, up_gradient
    )
    return (
        values,
        updated_down_weight,
        updated_up_weight,
        updated_down_first,
        updated_down_second,
        updated_up_first,
        updated_up_second,
    )


N = 4
RANK = 64
HALF = 128
CHUNK = 64
ROWS_STEP = 416
COL_STEP = 256
NT = (((1,), (1,)), ((), ()))
NN = (((1,), (0,)), ((), ()))
TN = (((0,), (0,)), ((), ()))


def fused_kernel(
    owners_ref,
    position_ref,
    x_ref,
    v_ref,
    dw_ref,
    uw_ref,
    dm_ref,
    ds_ref,
    um_ref,
    us_ref,
    g_ref,
    values_ref,
    ndw_ref,
    nuw_ref,
    ndm_ref,
    nds_ref,
    num_ref,
    nus_ref,
    line,
    uall,
    other,
    psend,
    prec,
    own_base,
    bpart,
    lpart,
    back_half,
    low_half,
    acc,
    csend,
    crecv,
    esend,
    erecv,
    extra,
    send_a,
    recv_a,
    send_z,
    recv_z,
    send_y,
    recv_y,
    send_p,
    recv_p,
    send_b,
    recv_b,
    send_l,
    recv_l,
    send_c,
    recv_c,
    send_e,
    recv_e,
):
    grp = lax.axis_index("groups")
    z = lax.axis_index("fsdp")
    own = lax.axis_index("owner")
    tokens = x_ref.shape[0]
    blocks = tokens // BLOCK
    width = x_ref.shape[1]
    down_factor = 1.0 / math.sqrt(MODEL_WIDTH)
    up_factor = branch_scale / math.sqrt(RANK)
    bf = jnp.bfloat16
    f32 = jnp.float32

    def remote(src, dst, ssem, rsem, **where):
        return pltpu.make_async_remote_copy(
            src_ref=src,
            dst_ref=dst,
            send_sem=ssem,
            recv_sem=rsem,
            device_id=where,
            device_id_type=pl.DeviceIdType.MESH,
        )

    def mod(i):
        return lax.rem(i + N, N)

    uall[z] = uw_ref[0].astype(bf)
    line[z, 0] = dw_ref[0].astype(bf)
    for c in range(2):
        first = pl.multiple_of(grp * HALF + c * CHUNK, CHUNK)
        line[z, 1 + c] = v_ref[pl.ds(first, CHUNK), :]
        first = pl.multiple_of((1 - grp) * HALF + c * CHUNK, CHUNK)
        other[z, c] = v_ref[pl.ds(first, CHUNK), :]

    barrier = pltpu.get_barrier_semaphore()
    for k in range(1, N):
        pl.semaphore_signal(
            barrier, inc=1, device_id={"fsdp": mod(z + k)}, device_id_type=pl.DeviceIdType.MESH
        )
        pl.semaphore_signal(
            barrier, inc=1, device_id={"owner": mod(own + k)}, device_id_type=pl.DeviceIdType.MESH
        )
    pl.semaphore_signal(
        barrier, inc=1, device_id={"groups": 1 - grp}, device_id_type=pl.DeviceIdType.MESH
    )
    pl.semaphore_wait(barrier, 7)

    def copy_a(k):
        return remote(
            uall.at[z], uall.at[z], send_a.at[k - 1], recv_a.at[k - 1], fsdp=mod(z + k)
        )

    def copy_z(s, kind, way):
        return remote(
            line.at[s, kind],
            line.at[s, kind],
            send_z.at[s, kind, way],
            recv_z.at[s, kind],
            fsdp=mod(z - 1 + 2 * way),
        )

    def copy_y(s, c):
        return remote(
            line.at[s, 1 + c],
            other.at[s, c],
            send_y.at[s, c],
            recv_y.at[s, c],
            groups=1 - grp,
        )

    def copy_p(s, h):
        k = mod(s - own)
        return remote(
            psend.at[s, h], prec.at[h, k - 1], send_p.at[s, h], recv_p.at[h, k - 1], owner=s
        )

    def copy_b(k):
        return remote(
            bpart.at[0], bpart.at[k], send_b.at[k - 1], recv_b.at[k - 1], owner=mod(own + k)
        )

    def copy_l(k):
        return remote(
            lpart.at[0], lpart.at[k], send_l.at[k - 1], recv_l.at[k - 1], owner=mod(own + k)
        )

    def copy_c(k):
        to = mod(z + k)
        return remote(
            csend.at[to], crecv.at[k - 1], send_c.at[k - 1], recv_c.at[k - 1], fsdp=to
        )

    def copy_e(k):
        to = mod(z + k)
        return remote(
            esend.at[to], erecv.at[k - 1], send_e.at[k - 1], recv_e.at[k - 1], fsdp=to
        )

    for k in range(1, N):
        copy_a(k).start()
    for kind in range(3):
        for way in range(2):

            @pl.when((z > 0) if way == 0 else (z < N - 1))
            def _():
                copy_z(z, kind, way).start()

    def product(s, mine):
        h = grp if mine else 1 - grp
        if mine:
            rows = line[s, 1:3].reshape(HALF, width)
        else:
            rows = other[s].reshape(HALF, width)

        @pl.loop(0, tokens // ROWS_STEP)
        def _(i):
            at = pl.ds(pl.multiple_of(i * ROWS_STEP, ROWS_STEP), ROWS_STEP)
            part = lax.dot_general(x_ref[at, :], rows, NT, preferred_element_type=f32)

            @pl.when(s == own)
            def _():
                own_base[h, at, :] = part

            @pl.when(s != own)
            def _():
                psend[s, h, at, :] = part.astype(bf)

        @pl.when(s != own)
        def _():
            copy_p(s, h).start()

    def sources(d):
        return ((z + d, z + d < N, 0), (z - d, z - d >= 0, 1))

    def forward(d):
        for kind in range(3):
            for s, valid, way in sources(d):

                @pl.when(valid)
                def _():
                    copy_z(s, kind, way).wait_recv()
                    if d < N - 1:

                        @pl.when((z > 0) if way == 0 else (z < N - 1))
                        def _():
                            copy_z(s, kind, way).start()

                    if kind > 0:
                        copy_y(s, kind - 1).start()

    def line_products(d):
        for s, valid, way in sources(d):

            @pl.when(valid)
            def _():
                product(s, True)

    def cross_products(d):
        for s, valid, way in sources(d):

            @pl.when(valid)
            def _():
                copy_y(s, 0).wait_recv()
                copy_y(s, 1).wait_recv()
                product(s, False)

    def block_rows(b):
        return pl.ds(pl.multiple_of(b * BLOCK, BLOCK), BLOCK)

    product(z, True)

    for k in range(1, N):
        copy_a(k).wait_recv()

    @pl.loop(0, blocks)
    def _(b):
        part = lax.dot_general(
            uall[owners_ref[b]], g_ref[block_rows(b), :], NT, preferred_element_type=f32
        )
        bpart[0, b] = (part * up_factor).astype(bf)

    for k in range(1, N):
        copy_b(k).start()
    product(z, False)
    for k in range(1, N):
        copy_b(k).wait_recv()

    @pl.loop(0, blocks)
    def _(b):
        total = (bpart[0, b].astype(f32) + bpart[1, b].astype(f32)) + (
            bpart[2, b].astype(f32) + bpart[3, b].astype(f32)
        )
        back_half[b] = total.astype(bf)

    @pl.loop(0, width // COL_STEP)
    def _(i):
        at = pl.ds(pl.multiple_of(i * COL_STEP, COL_STEP), COL_STEP)
        for p in range(N):
            total = None
            for b in range(p, blocks, N):
                part = lax.dot_general(
                    back_half[b],
                    x_ref[b * BLOCK : (b + 1) * BLOCK, at],
                    NN,
                    preferred_element_type=f32,
                )
                total = part if total is None else total + part
            acc[p, :, at] = (total * down_factor).astype(bf)

    for f in range(N):
        csend[f] = acc[position_ref[f]]

    forward(1)
    line_products(1)
    forward(2)
    line_products(2)
    cross_products(1)
    forward(3)
    for k in range(1, N):
        copy_c(k).start()

    @pl.loop(0, blocks)
    def _(b):
        part = lax.dot_general(
            line[owners_ref[b], 0], x_ref[block_rows(b), :], NT, preferred_element_type=f32
        )
        lpart[0, b] = (part * down_factor).astype(bf)

    for k in range(1, N):
        copy_l(k).start()
    line_products(3)
    cross_products(2)
    for k in range(1, N):
        copy_l(k).wait_recv()

    @pl.loop(0, blocks)
    def _(b):
        total = (lpart[0, b].astype(f32) + lpart[1, b].astype(f32)) + (
            lpart[2, b].astype(f32) + lpart[3, b].astype(f32)
        )
        half = total.astype(bf)
        low_half[b] = half
        extra[block_rows(b), :] = up_factor * lax.dot_general(
            half, uall[owners_ref[b]], TN, preferred_element_type=f32
        )

    for p in range(N):
        total = None
        for b in range(p, blocks, N):
            part = lax.dot_general(
                low_half[b],
                g_ref[b * BLOCK : (b + 1) * BLOCK, :],
                NN,
                preferred_element_type=f32,
            )
            total = part if total is None else total + part
        acc[p, :, 0:256] = (total * up_factor).astype(bf)
    for f in range(N):
        esend[f] = acc[position_ref[f], :, 0:256]
    for k in range(1, N):
        copy_e(k).start()
    cross_products(3)

    for k in range(1, N):
        copy_e(k).wait_recv()
    gradient = (esend[z].astype(f32) + erecv[0].astype(f32)) + (
        erecv[1].astype(f32) + erecv[2].astype(f32)
    )
    nuw_ref[0], num_ref[0], nus_ref[0] = adam_weight_update(
        uw_ref[0], um_ref[0], us_ref[0], gradient
    )
    for k in range(1, N):
        copy_c(k).wait_recv()

    @pl.loop(0, width // COL_STEP)
    def _(i):
        at = pl.ds(pl.multiple_of(i * COL_STEP, COL_STEP), COL_STEP)
        total = (csend[z, :, at].astype(f32) + crecv[0, :, at].astype(f32)) + (
            crecv[1, :, at].astype(f32) + crecv[2, :, at].astype(f32)
        )
        ndw_ref[0, :, at], ndm_ref[0, :, at], nds_ref[0, :, at] = adam_weight_update(
            dw_ref[0, :, at], dm_ref[0, :, at], ds_ref[0, :, at], total
        )

    for h in range(2):
        for k in range(1, N):
            remote(
                psend.at[0, h], prec.at[h, k - 1], send_p.at[0, h], recv_p.at[h, k - 1], owner=mod(own + k)
            ).wait_recv()
        cols = slice(h * HALF, (h + 1) * HALF)

        @pl.loop(0, tokens // ROWS_STEP)
        def _(i):
            at = pl.ds(pl.multiple_of(i * ROWS_STEP, ROWS_STEP), ROWS_STEP)
            total = (own_base[h, at, :] + prec[h, 0, at, :].astype(f32)) + (
                prec[h, 1, at, :].astype(f32) + prec[h, 2, at, :].astype(f32)
            )
            values_ref[at, cols] = (total + extra[at, cols]).astype(bf)

    for k in range(1, N):
        copy_a(k).wait_send()
        copy_b(k).wait_send()
        copy_l(k).wait_send()
        copy_c(k).wait_send()
        copy_e(k).wait_send()
    for kind in range(3):
        for way in range(2):
            room = (z > 0) if way == 0 else (z < N - 1)

            @pl.when(room)
            def _():
                copy_z(z, kind, way).wait_send()

            for d in range(1, N - 1):
                s, valid, _ = sources(d)[way]

                @pl.when(valid & room)
                def _():
                    copy_z(s, kind, way).wait_send()

    for k in range(1, N):
        for c in range(2):
            copy_y(mod(z + k), c).wait_send()
            copy_p(mod(own + k), c).wait_send()


def per_device_fused(
    inputs,
    value_matrix,
    adapter_down_weight,
    adapter_up_weight,
    down_first_moment,
    down_second_moment,
    up_first_moment,
    up_second_moment,
    output_gradient,
    tenant_of_block,
    tenant_storage_slot,
):
    my_index = lax.axis_index("fsdp")
    tokens, width = inputs.shape
    blocks = tokens // BLOCK
    tenants = lax.dynamic_slice_in_dim(tenant_of_block, my_index * blocks, blocks)
    ids = jnp.arange(N, dtype=jnp.int32)
    owners = jnp.sum(
        jnp.where(tenants[:, None] == ids[None, :], tenant_storage_slot[None, :], 0), axis=1
    )
    position = jnp.sum(
        jnp.where(owners[None, :N] == ids[:, None], ids[None, :], 0), axis=1
    )
    bf, f32 = jnp.bfloat16, jnp.float32
    big = jax.ShapeDtypeStruct((1, RANK, width), f32)
    small = jax.ShapeDtypeStruct((1, RANK, 256), f32)
    dma = pltpu.SemaphoreType.DMA
    vmem = pl.BlockSpec(memory_space=pltpu.VMEM)
    smem = pl.BlockSpec(memory_space=pltpu.SMEM)
    values, ndw, nuw, ndm, nds, num, nus = pl.pallas_call(
        fused_kernel,
        out_shape=(
            jax.ShapeDtypeStruct((tokens, 256), bf),
            big,
            small,
            big,
            big,
            small,
            small,
        ),
        in_specs=[smem] * 2 + [vmem] * 9,
        out_specs=[vmem] * 7,
        scratch_shapes=[
            pltpu.VMEM((N, 3, CHUNK, width), bf),
            pltpu.VMEM((N, RANK, 256), bf),
            pltpu.VMEM((N, 2, CHUNK, width), bf),
            pltpu.VMEM((N, 2, tokens, HALF), bf),
            pltpu.VMEM((2, 3, tokens, HALF), bf),
            pltpu.VMEM((2, tokens, HALF), f32),
            pltpu.VMEM((N, blocks, RANK, BLOCK), bf),
            pltpu.VMEM((N, blocks, RANK, BLOCK), bf),
            pltpu.VMEM((blocks, RANK, BLOCK), bf),
            pltpu.VMEM((blocks, RANK, BLOCK), bf),
            pltpu.VMEM((N, RANK, width), bf),
            pltpu.VMEM((N, RANK, width), bf),
            pltpu.VMEM((N - 1, RANK, width), bf),
            pltpu.VMEM((N, RANK, 256), bf),
            pltpu.VMEM((N - 1, RANK, 256), bf),
            pltpu.VMEM((tokens, 256), f32),
            dma((3,)),
            dma((3,)),
            dma((N, 3, 2)),
            dma((N, 3)),
            dma((N, 2)),
            dma((N, 2)),
            dma((N, 2)),
            dma((2, 3)),
            dma((3,)),
            dma((3,)),
            dma((3,)),
            dma((3,)),
            dma((3,)),
            dma((3,)),
            dma((3,)),
            dma((3,)),
        ],
        compiler_params=pltpu.CompilerParams(
            collective_id=0, has_side_effects=True, vmem_limit_bytes=56 * 1024 * 1024
        ),
    )(
        owners,
        position,
        inputs,
        value_matrix,
        adapter_down_weight,
        adapter_up_weight,
        down_first_moment,
        down_second_moment,
        up_first_moment,
        up_second_moment,
        output_gradient,
    )
    return values, ndw, nuw, ndm, nds, num, nus


def solution(mesh):
    sizes = mesh.shape
    fused = sizes["groups"] == 2 and sizes["fsdp"] == N and sizes["owner"] == N
    in_specs = (
        P(("groups", "fsdp"), "owner"),
        P("fsdp", "owner"),
        P(("groups", "fsdp"), None, "owner"),
        P(("groups", "fsdp"), None, "owner"),
        P(("groups", "fsdp"), None, "owner"),
        P(("groups", "fsdp"), None, "owner"),
        P(("groups", "fsdp"), None, "owner"),
        P(("groups", "fsdp"), None, "owner"),
        P(("groups", "fsdp"), "owner"),
        P("groups"),
        P("groups"),
    )
    out_specs = (
        P(("groups", "fsdp"), "owner"),
        P(("groups", "fsdp"), None, "owner"),
        P(("groups", "fsdp"), None, "owner"),
        P(("groups", "fsdp"), None, "owner"),
        P(("groups", "fsdp"), None, "owner"),
        P(("groups", "fsdp"), None, "owner"),
        P(("groups", "fsdp"), None, "owner"),
    )
    return jax.shard_map(
        per_device_fused if fused else per_device, mesh=mesh, in_specs=in_specs, out_specs=out_specs, check_vma=False
    )
```

```python
import math

import jax
import jax.numpy as jnp
from jax import lax
from jax.experimental import pallas as pl
from jax.experimental.pallas import tpu as pltpu
from jax.sharding import PartitionSpec as P

MODEL_WIDTH = 8192
BLOCK = 128


branch_scale = 0.5
first_moment = 0.9
second_moment = 0.999
learning_rate = 0.05
decay_rate = 0.01
epsilon = 1e-08
first_correction = 1.0 - math.exp(100.0 * math.log(0.9))
second_correction = 1.0 - math.exp(100.0 * math.log(0.999))


def adam_weight_update(weights, moment, second, gradient):
    new_moment = first_moment * moment + (1.0 - first_moment) * gradient
    new_second = second_moment * second + (1.0 - second_moment) * gradient * gradient
    direction = new_moment / first_correction / (jnp.sqrt(new_second / second_correction) + epsilon)
    new_weights = weights - learning_rate * (direction + decay_rate * weights)
    return (new_weights, new_moment, new_second)


def base_product(inputs, value_matrix):
    return jnp.einsum(
        "tk,jk->tj",
        inputs,
        lax.all_gather(value_matrix, "fsdp", axis=0, tiled=True),
        preferred_element_type=jnp.float32,
    )


def finish_values(base_values, low, block_up, up_factor):
    low_half = low.astype(jnp.bfloat16)
    extra = (
        jnp.einsum("brt,brj->btj", low_half, block_up, preferred_element_type=jnp.float32)
        * up_factor
    )
    return (low_half, (base_values + extra.reshape(base_values.shape)).astype(jnp.bfloat16))


def per_device(
    inputs,
    value_matrix,
    adapter_down_weight,
    adapter_up_weight,
    down_first_moment,
    down_second_moment,
    up_first_moment,
    up_second_moment,
    output_gradient,
    tenant_of_block,
    tenant_storage_slot,
):
    highest = lax.Precision.HIGHEST
    bin_count = lax.axis_size("fsdp")
    my_index = lax.axis_index("fsdp")
    tok_rows, quarter = inputs.shape
    block_count = tok_rows // BLOCK
    per_worker_share = adapter_down_weight.shape[0]
    adapter_rank_size = adapter_down_weight.shape[1]
    column_portion = adapter_up_weight.shape[2]
    adapter_count = tenant_storage_slot.shape[0]
    tenant_ids = jnp.arange(adapter_count, dtype=jnp.int32)
    slot_of_block = jnp.sum(
        jnp.where(tenant_of_block[:, None] == tenant_ids[None, :], tenant_storage_slot[None, :], 0),
        axis=1,
    )
    slot_grid = slot_of_block.reshape(bin_count, block_count)
    owner_grid = slot_grid // per_worker_share
    local_grid = slot_grid % per_worker_share
    local_ids = jnp.arange(per_worker_share, dtype=jnp.int32)
    wanted = jnp.any(
        (owner_grid[:, :, None] == my_index) & (local_grid[:, :, None] == local_ids[None, None, :]),
        axis=1,
    )
    chosen = wanted.astype(jnp.bfloat16)
    down_portion = adapter_down_weight.astype(jnp.bfloat16)
    up_portion = adapter_up_weight.astype(jnp.bfloat16)
    my_owners = lax.dynamic_index_in_dim(owner_grid, my_index, 0, keepdims=False)
    partial_value = base_product(inputs, value_matrix)
    send_down = jnp.einsum(
        "fj,jrk->frk", chosen, down_portion, preferred_element_type=jnp.float32
    ).astype(jnp.bfloat16)
    send_up = jnp.einsum(
        "fj,jrk->frk", chosen, up_portion, preferred_element_type=jnp.float32
    ).astype(jnp.bfloat16)
    arrived_down, arrived_up = (
        lax.all_to_all(send_down, "fsdp", split_axis=0, concat_axis=0, tiled=True),
        lax.all_to_all(send_up, "fsdp", split_axis=0, concat_axis=0, tiled=True),
    )
    block_down = jnp.take(arrived_down, my_owners, axis=0)
    block_up = jnp.take(arrived_up, my_owners, axis=0)
    row_blocks = inputs.reshape(block_count, BLOCK, quarter)
    grad_blocks = output_gradient.reshape(block_count, BLOCK, column_portion)
    down_factor = 1.0 / math.sqrt(MODEL_WIDTH)
    up_factor = branch_scale / math.sqrt(adapter_rank_size)
    low_part = (
        jnp.einsum("brk,btk->brt", block_down, row_blocks, preferred_element_type=jnp.float32)
        * down_factor
    )
    back_part = (
        jnp.einsum("btj,brj->brt", grad_blocks, block_up, preferred_element_type=jnp.float32)
        * up_factor
    )
    base_values = lax.psum_scatter(partial_value, "owner", scatter_dimension=1, tiled=True)
    low = lax.psum(low_part, "owner")
    low_half, values = finish_values(base_values, low, block_up, up_factor)
    back = lax.psum(back_part.astype(jnp.bfloat16), "owner")
    up_blocks = (
        jnp.einsum("brt,btj->brj", low_half, grad_blocks, preferred_element_type=jnp.float32)
        * up_factor
    )
    down_blocks = (
        jnp.einsum("brt,btk->brk", back, row_blocks, preferred_element_type=jnp.float32)
        * down_factor
    )
    route = (my_owners[:, None] == jnp.arange(bin_count, dtype=jnp.int32)[None, :]).astype(
        jnp.float32
    )
    back_down = jnp.einsum("bg,brk->grk", route, down_blocks, precision=highest).astype(
        jnp.bfloat16
    )
    back_up = jnp.einsum("bg,brj->grj", route, up_blocks, precision=highest).astype(jnp.bfloat16)
    returned_down, returned_up = (
        lax.all_to_all(back_down, "fsdp", split_axis=0, concat_axis=0, tiled=True),
        lax.all_to_all(back_up, "fsdp", split_axis=0, concat_axis=0, tiled=True),
    )
    down_gradient = jnp.einsum(
        "fj,frk->jrk", chosen, returned_down, preferred_element_type=jnp.float32
    )
    up_gradient = jnp.einsum("fj,frk->jrk", chosen, returned_up, preferred_element_type=jnp.float32)
    updated_down_weight, updated_down_first, updated_down_second = adam_weight_update(
        adapter_down_weight, down_first_moment, down_second_moment, down_gradient
    )
    updated_up_weight, updated_up_first, updated_up_second = adam_weight_update(
        adapter_up_weight, up_first_moment, up_second_moment, up_gradient
    )
    return (
        values,
        updated_down_weight,
        updated_up_weight,
        updated_down_first,
        updated_down_second,
        updated_up_first,
        updated_up_second,
    )


N = 4
RANK = 64
HALF = 128
CHUNK = 64
ROWS_STEP = 416
COL_STEP = 256
NT = (((1,), (1,)), ((), ()))
NN = (((1,), (0,)), ((), ()))
TN = (((0,), (0,)), ((), ()))


def fused_kernel(
    tenant_ref,
    storage_ref,
    x_hbm,
    v_ref,
    dw_ref,
    uw_ref,
    g_hbm,
    values_ref,
    grad_down_ref,
    grad_up_ref,
    x_ref,
    g_ref,
    dall,
    line,
    uall,
    other,
    psend,
    prec,
    own_base,
    bpart,
    lpart,
    back_half,
    low_half,
    acc,
    csend,
    crecv,
    esend,
    erecv,
    extra,
    send_a,
    recv_a,
    send_z,
    recv_z,
    send_y,
    recv_y,
    send_p,
    recv_p,
    send_b,
    recv_b,
    send_l,
    recv_l,
    send_c,
    recv_c,
    send_e,
    recv_e,
    load_sem,
):
    grp = lax.axis_index("groups")
    z = lax.axis_index("fsdp")
    own = lax.axis_index("owner")
    tokens = x_ref.shape[0]
    blocks = tokens // BLOCK
    width = x_ref.shape[1]
    down_factor = 1.0 / math.sqrt(MODEL_WIDTH)
    up_factor = branch_scale / math.sqrt(RANK)
    bf = jnp.bfloat16
    f32 = jnp.float32

    load_g = pltpu.make_async_copy(g_hbm, g_ref, load_sem.at[0])
    load_x = pltpu.make_async_copy(x_hbm, x_ref, load_sem.at[1])
    load_g.start()
    load_x.start()

    def owner_of(b):
        return storage_ref[tenant_ref[z * blocks + b]]

    def position_of(f):
        place = 0
        for p in range(1, N):
            place = jnp.where(owner_of(p) == f, p, place)
        return place

    def remote(src, dst, ssem, rsem, **where):
        return pltpu.make_async_remote_copy(
            src_ref=src,
            dst_ref=dst,
            send_sem=ssem,
            recv_sem=rsem,
            device_id=where,
            device_id_type=pl.DeviceIdType.MESH,
        )

    def mod(i):
        return lax.rem(i + N, N)

    uall[z] = uw_ref[0].astype(bf)
    dall[z] = dw_ref[0].astype(bf)
    for c in range(2):
        first = pl.multiple_of(grp * HALF + c * CHUNK, CHUNK)
        line[z, c] = v_ref[pl.ds(first, CHUNK), :]
        first = pl.multiple_of((1 - grp) * HALF + c * CHUNK, CHUNK)
        other[z, c] = v_ref[pl.ds(first, CHUNK), :]

    barrier = pltpu.get_barrier_semaphore()
    for k in range(1, N):
        pl.semaphore_signal(
            barrier, inc=1, device_id={"fsdp": mod(z + k)}, device_id_type=pl.DeviceIdType.MESH
        )
        pl.semaphore_signal(
            barrier, inc=1, device_id={"owner": mod(own + k)}, device_id_type=pl.DeviceIdType.MESH
        )
    pl.semaphore_signal(
        barrier, inc=1, device_id={"groups": 1 - grp}, device_id_type=pl.DeviceIdType.MESH
    )
    pl.semaphore_wait(barrier, 7)

    def copy_a(k):
        return remote(
            uall.at[z], uall.at[z], send_a.at[k - 1], recv_a.at[k - 1], fsdp=mod(z + k)
        )

    def copy_z(s, kind, way):
        piece = dall.at[s] if kind == 0 else line.at[s, kind - 1]
        return remote(
            piece,
            piece,
            send_z.at[s, kind, way],
            recv_z.at[s, kind],
            fsdp=mod(z - 1 + 2 * way),
        )

    def copy_y(s, c):
        return remote(
            line.at[s, c],
            other.at[s, c],
            send_y.at[s, c],
            recv_y.at[s, c],
            groups=1 - grp,
        )

    def copy_p(s, h):
        k = mod(s - own)
        return remote(
            psend.at[s, h], prec.at[h, k - 1], send_p.at[s, h], recv_p.at[h, k - 1], owner=s
        )

    def copy_b(k):
        return remote(
            bpart.at[0], bpart.at[k], send_b.at[k - 1], recv_b.at[k - 1], owner=mod(own + k)
        )

    def copy_l(k):
        return remote(
            lpart.at[0], lpart.at[k], send_l.at[k - 1], recv_l.at[k - 1], owner=mod(own + k)
        )

    def copy_c(k):
        to = mod(z + k)
        return remote(
            csend.at[to], crecv.at[k - 1], send_c.at[k - 1], recv_c.at[k - 1], fsdp=to
        )

    def copy_e(k):
        to = mod(z + k)
        return remote(
            esend.at[to], erecv.at[k - 1], send_e.at[k - 1], recv_e.at[k - 1], fsdp=to
        )

    for k in range(1, N):
        copy_a(k).start()

    def send_own(kind):
        for way in range(2):

            @pl.when((z > 0) if way == 0 else (z < N - 1))
            def _():
                copy_z(z, kind, way).start()

    send_own(0)
    send_own(1)

    def product(s, mine):
        h = grp if mine else 1 - grp
        if mine:
            rows = line[s].reshape(HALF, width)
        else:
            rows = other[s].reshape(HALF, width)

        @pl.loop(0, tokens // ROWS_STEP)
        def _(i):
            at = pl.ds(pl.multiple_of(i * ROWS_STEP, ROWS_STEP), ROWS_STEP)
            part = lax.dot_general(x_ref[at, :], rows, NT, preferred_element_type=f32)

            @pl.when(s == own)
            def _():
                own_base[h, at, :] = part

            @pl.when(s != own)
            def _():
                psend[s, h, at, :] = part.astype(bf)

        @pl.when(s != own)
        def _():
            copy_p(s, h).start()

    def sources(d):
        return ((z + d, z + d < N, 0), (z - d, z - d >= 0, 1))

    def forward(d, kind):
        for s, valid, way in sources(d):

            @pl.when(valid)
            def _():
                copy_z(s, kind, way).wait_recv()
                if d < N - 1:

                    @pl.when((z > 0) if way == 0 else (z < N - 1))
                    def _():
                        copy_z(s, kind, way).start()

                if kind > 0:
                    copy_y(s, kind - 1).start()

    def sent_forward(d, kind):
        for s, valid, way in sources(d):

            @pl.when(valid & ((z > 0) if way == 0 else (z < N - 1)))
            def _():
                copy_z(s, kind, way).wait_send()

    def line_products(d):
        for s, valid, way in sources(d):

            @pl.when(valid)
            def _():
                product(s, True)

    def cross_products(d):
        for s, valid, way in sources(d):

            @pl.when(valid)
            def _():
                copy_y(s, 0).wait_recv()
                copy_y(s, 1).wait_recv()
                product(s, False)

    def block_rows(b):
        return pl.ds(pl.multiple_of(b * BLOCK, BLOCK), BLOCK)

    load_g.wait()
    for k in range(1, N):
        copy_a(k).wait_recv()

    @pl.loop(0, blocks)
    def _(b):
        part = lax.dot_general(
            uall[owner_of(b)], g_ref[block_rows(b), :], NT, preferred_element_type=f32
        )
        bpart[0, b] = (part * up_factor).astype(bf)

    for k in range(1, N):
        copy_b(k).start()
    load_x.wait()
    product(z, True)
    forward(1, 0)
    send_own(2)
    product(z, False)
    for k in range(1, N):
        copy_b(k).wait_recv()

    @pl.loop(0, blocks)
    def _(b):
        total = (bpart[0, b].astype(f32) + bpart[1, b].astype(f32)) + (
            bpart[2, b].astype(f32) + bpart[3, b].astype(f32)
        )
        back_half[b] = total.astype(bf)

    @pl.loop(0, width // COL_STEP)
    def _(i):
        at = pl.ds(pl.multiple_of(i * COL_STEP, COL_STEP), COL_STEP)
        for p in range(N):
            total = None
            for b in range(p, blocks, N):
                part = lax.dot_general(
                    back_half[b],
                    x_ref[b * BLOCK : (b + 1) * BLOCK, at],
                    NN,
                    preferred_element_type=f32,
                )
                total = part if total is None else total + part
            acc[p, :, at] = (total * down_factor).astype(bf)

    for f in range(N):
        csend[f] = acc[position_of(f)]

    forward(2, 0)
    forward(1, 1)
    forward(1, 2)
    line_products(1)
    forward(3, 0)
    forward(2, 1)
    @pl.loop(0, blocks)
    def _(b):
        part = lax.dot_general(
            dall[owner_of(b)], x_ref[block_rows(b), :], NT, preferred_element_type=f32
        )
        lpart[0, b] = (part * down_factor).astype(bf)

    for k in range(1, N):
        copy_l(k).start()
    forward(2, 2)
    line_products(2)
    cross_products(1)
    for k in range(1, N):
        copy_l(k).wait_recv()

    @pl.loop(0, blocks)
    def _(b):
        total = (lpart[0, b].astype(f32) + lpart[1, b].astype(f32)) + (
            lpart[2, b].astype(f32) + lpart[3, b].astype(f32)
        )
        half = total.astype(bf)
        low_half[b] = half
        extra[block_rows(b), :] = up_factor * lax.dot_general(
            half, uall[owner_of(b)], TN, preferred_element_type=f32
        )

    for p in range(N):
        total = None
        for b in range(p, blocks, N):
            part = lax.dot_general(
                low_half[b],
                g_ref[b * BLOCK : (b + 1) * BLOCK, :],
                NN,
                preferred_element_type=f32,
            )
            total = part if total is None else total + part
        acc[p, :, 0:256] = (total * up_factor).astype(bf)
    for f in range(N):
        esend[f] = acc[position_of(f), :, 0:256]
    for k in range(1, N):
        copy_e(k).start()
    forward(3, 1)
    forward(3, 2)
    for kind in (1, 2):
        sent_forward(2, kind)
    for k in range(1, N):
        copy_c(k).start()
    line_products(3)
    cross_products(2)
    cross_products(3)

    for k in range(1, N):
        copy_e(k).wait_recv()
    grad_up_ref[0] = (esend[z].astype(f32) + erecv[0].astype(f32)) + (
        erecv[1].astype(f32) + erecv[2].astype(f32)
    )
    for k in range(1, N):
        copy_c(k).wait_recv()

    @pl.loop(0, width // COL_STEP)
    def _(i):
        at = pl.ds(pl.multiple_of(i * COL_STEP, COL_STEP), COL_STEP)
        grad_down_ref[0, :, at] = (csend[z, :, at].astype(f32) + crecv[0, :, at].astype(f32)) + (
            crecv[1, :, at].astype(f32) + crecv[2, :, at].astype(f32)
        )

    for h in range(2):
        for k in range(1, N):
            remote(
                psend.at[0, h], prec.at[h, k - 1], send_p.at[0, h], recv_p.at[h, k - 1], owner=mod(own + k)
            ).wait_recv()
        cols = slice(h * HALF, (h + 1) * HALF)

        @pl.loop(0, tokens // ROWS_STEP)
        def _(i):
            at = pl.ds(pl.multiple_of(i * ROWS_STEP, ROWS_STEP), ROWS_STEP)
            total = (own_base[h, at, :] + prec[h, 0, at, :].astype(f32)) + (
                prec[h, 1, at, :].astype(f32) + prec[h, 2, at, :].astype(f32)
            )
            values_ref[at, cols] = total + extra[at, cols]

    for k in range(1, N):
        copy_a(k).wait_send()
        copy_b(k).wait_send()
        copy_l(k).wait_send()
        copy_c(k).wait_send()
        copy_e(k).wait_send()
    for kind in range(3):
        for way in range(2):
            room = (z > 0) if way == 0 else (z < N - 1)

            @pl.when(room)
            def _():
                copy_z(z, kind, way).wait_send()

        sent_forward(1, kind)
    sent_forward(2, 0)

    for k in range(1, N):
        for c in range(2):
            copy_y(mod(z + k), c).wait_send()
            copy_p(mod(own + k), c).wait_send()


def per_device_fused(
    inputs,
    value_matrix,
    adapter_down_weight,
    adapter_up_weight,
    down_first_moment,
    down_second_moment,
    up_first_moment,
    up_second_moment,
    output_gradient,
    tenant_of_block,
    tenant_storage_slot,
):
    tokens, width = inputs.shape
    blocks = tokens // BLOCK
    bf, f32 = jnp.bfloat16, jnp.float32
    big = jax.ShapeDtypeStruct((1, RANK, width), f32)
    small = jax.ShapeDtypeStruct((1, RANK, 256), f32)
    dma = pltpu.SemaphoreType.DMA
    vmem = pl.BlockSpec(memory_space=pltpu.VMEM)
    smem = pl.BlockSpec(memory_space=pltpu.SMEM)
    hbm = pl.BlockSpec(memory_space=pl.ANY)
    values, grad_down, grad_up = pl.pallas_call(
        fused_kernel,
        out_shape=(
            jax.ShapeDtypeStruct((tokens, 256), f32),
            big,
            small,
        ),
        in_specs=[smem, smem, hbm, vmem, vmem, vmem, hbm],
        out_specs=[vmem] * 3,
        scratch_shapes=[
            pltpu.VMEM((tokens, width), bf),
            pltpu.VMEM((tokens, 256), bf),
            pltpu.VMEM((N, RANK, width), bf),
            pltpu.VMEM((N, 2, CHUNK, width), bf),
            pltpu.VMEM((N, RANK, 256), bf),
            pltpu.VMEM((N, 2, CHUNK, width), bf),
            pltpu.VMEM((N, 2, tokens, HALF), bf),
            pltpu.VMEM((2, 3, tokens, HALF), bf),
            pltpu.VMEM((2, tokens, HALF), f32),
            pltpu.VMEM((N, blocks, RANK, BLOCK), bf),
            pltpu.VMEM((N, blocks, RANK, BLOCK), bf),
            pltpu.VMEM((blocks, RANK, BLOCK), bf),
            pltpu.VMEM((blocks, RANK, BLOCK), bf),
            pltpu.VMEM((N, RANK, width), bf),
            pltpu.VMEM((N, RANK, width), bf),
            pltpu.VMEM((N - 1, RANK, width), bf),
            pltpu.VMEM((N, RANK, 256), bf),
            pltpu.VMEM((N - 1, RANK, 256), bf),
            pltpu.VMEM((tokens, 256), f32),
            dma((3,)),
            dma((3,)),
            dma((N, 3, 2)),
            dma((N, 3)),
            dma((N, 2)),
            dma((N, 2)),
            dma((N, 2)),
            dma((2, 3)),
            dma((3,)),
            dma((3,)),
            dma((3,)),
            dma((3,)),
            dma((3,)),
            dma((3,)),
            dma((3,)),
            dma((3,)),
            dma((2,)),
        ],
        compiler_params=pltpu.CompilerParams(
            collective_id=0, has_side_effects=True, vmem_limit_bytes=56 * 1024 * 1024
        ),
    )(
        tenant_of_block,
        tenant_storage_slot,
        inputs,
        value_matrix,
        adapter_down_weight,
        adapter_up_weight,
        output_gradient,
    )
    ndw, ndm, nds = adam_weight_update(
        adapter_down_weight, down_first_moment, down_second_moment, grad_down
    )
    nuw, num, nus = adam_weight_update(
        adapter_up_weight, up_first_moment, up_second_moment, grad_up
    )
    return values.astype(bf), ndw, nuw, ndm, nds, num, nus


def solution(mesh):
    sizes = mesh.shape
    fused = sizes["groups"] == 2 and sizes["fsdp"] == N and sizes["owner"] == N
    in_specs = (
        P(("groups", "fsdp"), "owner"),
        P("fsdp", "owner"),
        P(("groups", "fsdp"), None, "owner"),
        P(("groups", "fsdp"), None, "owner"),
        P(("groups", "fsdp"), None, "owner"),
        P(("groups", "fsdp"), None, "owner"),
        P(("groups", "fsdp"), None, "owner"),
        P(("groups", "fsdp"), None, "owner"),
        P(("groups", "fsdp"), "owner"),
        P("groups"),
        P("groups"),
    )
    out_specs = (
        P(("groups", "fsdp"), "owner"),
        P(("groups", "fsdp"), None, "owner"),
        P(("groups", "fsdp"), None, "owner"),
        P(("groups", "fsdp"), None, "owner"),
        P(("groups", "fsdp"), None, "owner"),
        P(("groups", "fsdp"), None, "owner"),
        P(("groups", "fsdp"), None, "owner"),
    )
    return jax.shard_map(
        per_device_fused if fused else per_device, mesh=mesh, in_specs=in_specs, out_specs=out_specs, check_vma=False
    )
```

```python
import math

import jax
import jax.numpy as jnp
from jax import lax
from jax.experimental import pallas as pl
from jax.experimental.pallas import tpu as pltpu
from jax.sharding import PartitionSpec as P

MODEL_WIDTH = 8192
BLOCK = 128


branch_scale = 0.5
first_moment = 0.9
second_moment = 0.999
learning_rate = 0.05
decay_rate = 0.01
epsilon = 1e-08
first_correction = 1.0 - math.exp(100.0 * math.log(0.9))
second_correction = 1.0 - math.exp(100.0 * math.log(0.999))


def adam_weight_update(weights, moment, second, gradient):
    new_moment = first_moment * moment + (1.0 - first_moment) * gradient
    new_second = second_moment * second + (1.0 - second_moment) * gradient * gradient
    direction = new_moment / first_correction / (jnp.sqrt(new_second / second_correction) + epsilon)
    new_weights = weights - learning_rate * (direction + decay_rate * weights)
    return (new_weights, new_moment, new_second)


def base_product(inputs, value_matrix):
    return jnp.einsum(
        "tk,jk->tj",
        inputs,
        lax.all_gather(value_matrix, "fsdp", axis=0, tiled=True),
        preferred_element_type=jnp.float32,
    )


def finish_values(base_values, low, block_up, up_factor):
    low_half = low.astype(jnp.bfloat16)
    extra = (
        jnp.einsum("brt,brj->btj", low_half, block_up, preferred_element_type=jnp.float32)
        * up_factor
    )
    return (low_half, (base_values + extra.reshape(base_values.shape)).astype(jnp.bfloat16))


def per_device(
    inputs,
    value_matrix,
    adapter_down_weight,
    adapter_up_weight,
    down_first_moment,
    down_second_moment,
    up_first_moment,
    up_second_moment,
    output_gradient,
    tenant_of_block,
    tenant_storage_slot,
):
    highest = lax.Precision.HIGHEST
    bin_count = lax.axis_size("fsdp")
    my_index = lax.axis_index("fsdp")
    tok_rows, quarter = inputs.shape
    block_count = tok_rows // BLOCK
    per_worker_share = adapter_down_weight.shape[0]
    adapter_rank_size = adapter_down_weight.shape[1]
    column_portion = adapter_up_weight.shape[2]
    adapter_count = tenant_storage_slot.shape[0]
    tenant_ids = jnp.arange(adapter_count, dtype=jnp.int32)
    slot_of_block = jnp.sum(
        jnp.where(tenant_of_block[:, None] == tenant_ids[None, :], tenant_storage_slot[None, :], 0),
        axis=1,
    )
    slot_grid = slot_of_block.reshape(bin_count, block_count)
    owner_grid = slot_grid // per_worker_share
    local_grid = slot_grid % per_worker_share
    local_ids = jnp.arange(per_worker_share, dtype=jnp.int32)
    wanted = jnp.any(
        (owner_grid[:, :, None] == my_index) & (local_grid[:, :, None] == local_ids[None, None, :]),
        axis=1,
    )
    chosen = wanted.astype(jnp.bfloat16)
    down_portion = adapter_down_weight.astype(jnp.bfloat16)
    up_portion = adapter_up_weight.astype(jnp.bfloat16)
    my_owners = lax.dynamic_index_in_dim(owner_grid, my_index, 0, keepdims=False)
    partial_value = base_product(inputs, value_matrix)
    send_down = jnp.einsum(
        "fj,jrk->frk", chosen, down_portion, preferred_element_type=jnp.float32
    ).astype(jnp.bfloat16)
    send_up = jnp.einsum(
        "fj,jrk->frk", chosen, up_portion, preferred_element_type=jnp.float32
    ).astype(jnp.bfloat16)
    arrived_down, arrived_up = (
        lax.all_to_all(send_down, "fsdp", split_axis=0, concat_axis=0, tiled=True),
        lax.all_to_all(send_up, "fsdp", split_axis=0, concat_axis=0, tiled=True),
    )
    block_down = jnp.take(arrived_down, my_owners, axis=0)
    block_up = jnp.take(arrived_up, my_owners, axis=0)
    row_blocks = inputs.reshape(block_count, BLOCK, quarter)
    grad_blocks = output_gradient.reshape(block_count, BLOCK, column_portion)
    down_factor = 1.0 / math.sqrt(MODEL_WIDTH)
    up_factor = branch_scale / math.sqrt(adapter_rank_size)
    low_part = (
        jnp.einsum("brk,btk->brt", block_down, row_blocks, preferred_element_type=jnp.float32)
        * down_factor
    )
    back_part = (
        jnp.einsum("btj,brj->brt", grad_blocks, block_up, preferred_element_type=jnp.float32)
        * up_factor
    )
    base_values = lax.psum_scatter(partial_value, "owner", scatter_dimension=1, tiled=True)
    low = lax.psum(low_part, "owner")
    low_half, values = finish_values(base_values, low, block_up, up_factor)
    back = lax.psum(back_part.astype(jnp.bfloat16), "owner")
    up_blocks = (
        jnp.einsum("brt,btj->brj", low_half, grad_blocks, preferred_element_type=jnp.float32)
        * up_factor
    )
    down_blocks = (
        jnp.einsum("brt,btk->brk", back, row_blocks, preferred_element_type=jnp.float32)
        * down_factor
    )
    route = (my_owners[:, None] == jnp.arange(bin_count, dtype=jnp.int32)[None, :]).astype(
        jnp.float32
    )
    back_down = jnp.einsum("bg,brk->grk", route, down_blocks, precision=highest).astype(
        jnp.bfloat16
    )
    back_up = jnp.einsum("bg,brj->grj", route, up_blocks, precision=highest).astype(jnp.bfloat16)
    returned_down, returned_up = (
        lax.all_to_all(back_down, "fsdp", split_axis=0, concat_axis=0, tiled=True),
        lax.all_to_all(back_up, "fsdp", split_axis=0, concat_axis=0, tiled=True),
    )
    down_gradient = jnp.einsum(
        "fj,frk->jrk", chosen, returned_down, preferred_element_type=jnp.float32
    )
    up_gradient = jnp.einsum("fj,frk->jrk", chosen, returned_up, preferred_element_type=jnp.float32)
    updated_down_weight, updated_down_first, updated_down_second = adam_weight_update(
        adapter_down_weight, down_first_moment, down_second_moment, down_gradient
    )
    updated_up_weight, updated_up_first, updated_up_second = adam_weight_update(
        adapter_up_weight, up_first_moment, up_second_moment, up_gradient
    )
    return (
        values,
        updated_down_weight,
        updated_up_weight,
        updated_down_first,
        updated_down_second,
        updated_up_first,
        updated_up_second,
    )


N = 4
RANK = 64
HALF = 128
CHUNK = 64
ROWS_STEP = 416
COL_STEP = 256
NT = (((1,), (1,)), ((), ()))
NN = (((1,), (0,)), ((), ()))
TN = (((0,), (0,)), ((), ()))


def fused_kernel(
    tenant_ref,
    storage_ref,
    x_hbm,
    v_ref,
    dw_ref,
    uw_ref,
    g_hbm,
    values_ref,
    grad_down_ref,
    grad_up_ref,
    x_ref,
    g_ref,
    dall,
    line,
    uall,
    other,
    psend,
    prec,
    own_base,
    bpart,
    bpair,
    lpart,
    lpair,
    back_half,
    low_half,
    acc,
    csend,
    crecv,
    esend,
    erecv,
    extra,
    send_a,
    recv_a,
    send_z,
    recv_z,
    send_y,
    recv_y,
    send_p,
    recv_p,
    send_b,
    recv_b,
    send_l,
    recv_l,
    send_c,
    recv_c,
    send_e,
    recv_e,
    load_sem,
):
    grp = lax.axis_index("groups")
    z = lax.axis_index("fsdp")
    own = lax.axis_index("owner")
    tokens = x_ref.shape[0]
    blocks = tokens // BLOCK
    width = x_ref.shape[1]
    down_factor = 1.0 / math.sqrt(MODEL_WIDTH)
    up_factor = branch_scale / math.sqrt(RANK)
    bf = jnp.bfloat16
    f32 = jnp.float32

    load_g = pltpu.make_async_copy(g_hbm, g_ref, load_sem.at[0])
    load_x = pltpu.make_async_copy(x_hbm, x_ref, load_sem.at[1])
    load_g.start()
    load_x.start()

    def owner_of(b):
        return storage_ref[tenant_ref[z * blocks + b]]

    def position_of(f):
        place = 0
        for p in range(1, N):
            place = jnp.where(owner_of(p) == f, p, place)
        return place

    def remote(src, dst, ssem, rsem, **where):
        return pltpu.make_async_remote_copy(
            src_ref=src,
            dst_ref=dst,
            send_sem=ssem,
            recv_sem=rsem,
            device_id=where,
            device_id_type=pl.DeviceIdType.MESH,
        )

    def mod(i):
        return lax.rem(i + N, N)

    uall[z] = uw_ref[0].astype(bf)
    dall[z] = dw_ref[0].astype(bf)
    for c in range(2):
        first = pl.multiple_of(grp * HALF + c * CHUNK, CHUNK)
        line[z, c] = v_ref[pl.ds(first, CHUNK), :]
        first = pl.multiple_of((1 - grp) * HALF + c * CHUNK, CHUNK)
        other[z, c] = v_ref[pl.ds(first, CHUNK), :]

    barrier = pltpu.get_barrier_semaphore()
    for k in range(1, N):
        pl.semaphore_signal(
            barrier, inc=1, device_id={"fsdp": mod(z + k)}, device_id_type=pl.DeviceIdType.MESH
        )
        pl.semaphore_signal(
            barrier, inc=1, device_id={"owner": mod(own + k)}, device_id_type=pl.DeviceIdType.MESH
        )
    pl.semaphore_signal(
        barrier, inc=1, device_id={"groups": 1 - grp}, device_id_type=pl.DeviceIdType.MESH
    )
    pl.semaphore_wait(barrier, 7)

    def copy_a(k):
        return remote(
            uall.at[z], uall.at[z], send_a.at[k - 1], recv_a.at[k - 1], fsdp=mod(z + k)
        )

    def copy_z(s, kind, way):
        piece = dall.at[s] if kind == 0 else line.at[s, kind - 1]
        return remote(
            piece,
            piece,
            send_z.at[s, kind, way],
            recv_z.at[s, kind],
            fsdp=mod(z - 1 + 2 * way),
        )

    def copy_y(s, c):
        return remote(
            line.at[s, c],
            other.at[s, c],
            send_y.at[s, c],
            recv_y.at[s, c],
            groups=1 - grp,
        )

    def copy_p(s, h):
        k = mod(s - own)
        return remote(
            psend.at[s, h], prec.at[h, k - 1], send_p.at[s, h], recv_p.at[h, k - 1], owner=s
        )

    def copy_b(k):
        flip = 1 - 2 * lax.rem(own, 2) if k == 1 else 2 - 4 * (own // 2)
        part = bpart if k == 1 else bpair
        return remote(
            part.at[0], part.at[1], send_b.at[k - 1], recv_b.at[k - 1], owner=own + flip
        )

    def copy_l(k):
        flip = 1 - 2 * lax.rem(own, 2) if k == 1 else 2 - 4 * (own // 2)
        part = lpart if k == 1 else lpair
        return remote(
            part.at[0], part.at[1], send_l.at[k - 1], recv_l.at[k - 1], owner=own + flip
        )

    def copy_c(k):
        to = mod(z + k)
        return remote(
            csend.at[to], crecv.at[k - 1], send_c.at[k - 1], recv_c.at[k - 1], fsdp=to
        )

    def start_c(stage):
        for k in range(1, N):
            to = mod(z + k)

            @pl.when(jnp.where(to > z, to, N - 1 - to) == stage)
            def _():
                copy_c(k).start()

    def copy_e(k):
        to = mod(z + k)
        return remote(
            esend.at[to], erecv.at[k - 1], send_e.at[k - 1], recv_e.at[k - 1], fsdp=to
        )

    for k in range(1, N):
        copy_a(k).start()

    def send_own(kind):
        for way in range(2):

            @pl.when((z > 0) if way == 0 else (z < N - 1))
            def _():
                copy_z(z, kind, way).start()

    send_own(0)
    send_own(1)

    def product(s, mine):
        h = grp if mine else 1 - grp
        if mine:
            rows = line[s].reshape(HALF, width)
        else:
            rows = other[s].reshape(HALF, width)

        @pl.loop(0, tokens // ROWS_STEP)
        def _(i):
            at = pl.ds(pl.multiple_of(i * ROWS_STEP, ROWS_STEP), ROWS_STEP)
            part = lax.dot_general(x_ref[at, :], rows, NT, preferred_element_type=f32)

            @pl.when(s == own)
            def _():
                own_base[h, at, :] = part

            @pl.when(s != own)
            def _():
                psend[s, h, at, :] = part.astype(bf)

        @pl.when(s != own)
        def _():
            copy_p(s, h).start()

    def sources(d):
        return ((z + d, z + d < N, 0), (z - d, z - d >= 0, 1))

    def forward(d, kind):
        for s, valid, way in sources(d):

            @pl.when(valid)
            def _():
                copy_z(s, kind, way).wait_recv()
                if d < N - 1:

                    @pl.when((z > 0) if way == 0 else (z < N - 1))
                    def _():
                        copy_z(s, kind, way).start()

                if kind > 0:
                    copy_y(s, kind - 1).start()

    def sent_forward(d, kind):
        for s, valid, way in sources(d):

            @pl.when(valid & ((z > 0) if way == 0 else (z < N - 1)))
            def _():
                copy_z(s, kind, way).wait_send()

    def line_products(d):
        for s, valid, way in sources(d):

            @pl.when(valid)
            def _():
                product(s, True)

    def cross_products(d):
        for s, valid, way in sources(d):

            @pl.when(valid)
            def _():
                copy_y(s, 0).wait_recv()
                copy_y(s, 1).wait_recv()
                product(s, False)

    def block_rows(b):
        return pl.ds(pl.multiple_of(b * BLOCK, BLOCK), BLOCK)

    load_g.wait()
    for k in range(1, N):
        copy_a(k).wait_recv()

    @pl.loop(0, blocks)
    def _(b):
        part = lax.dot_general(
            uall[owner_of(b)], g_ref[block_rows(b), :], NT, preferred_element_type=f32
        )
        bpart[0, b] = part * up_factor

    copy_b(1).start()
    copy_b(1).wait_recv()
    bpair[0] = (bpart[0] + bpart[1]).astype(bf)
    copy_b(2).start()
    load_x.wait()
    product(z, True)
    forward(1, 0)
    send_own(2)
    product(z, False)
    copy_b(2).wait_recv()

    @pl.loop(0, blocks)
    def _(b):
        total = bpair[0, b].astype(f32) + bpair[1, b].astype(f32)
        back_half[b] = total.astype(bf)

    @pl.loop(0, width // COL_STEP)
    def _(i):
        at = pl.ds(pl.multiple_of(i * COL_STEP, COL_STEP), COL_STEP)
        for p in range(N):
            total = None
            for b in range(p, blocks, N):
                part = lax.dot_general(
                    back_half[b],
                    x_ref[b * BLOCK : (b + 1) * BLOCK, at],
                    NN,
                    preferred_element_type=f32,
                )
                total = part if total is None else total + part
            acc[p, :, at] = (total * down_factor).astype(bf)

    for f in range(N):
        csend[f] = acc[position_of(f)]
    start_c(1)

    forward(2, 0)
    forward(1, 1)
    forward(1, 2)
    line_products(1)
    forward(3, 0)
    forward(2, 1)
    @pl.loop(0, blocks)
    def _(b):
        part = lax.dot_general(
            dall[owner_of(b)], x_ref[block_rows(b), :], NT, preferred_element_type=f32
        )
        lpart[0, b] = part * down_factor

    copy_l(1).start()
    copy_l(1).wait_recv()
    lpair[0] = (lpart[0] + lpart[1]).astype(bf)
    copy_l(2).start()
    forward(2, 2)
    start_c(2)
    line_products(2)
    cross_products(1)
    cross_products(2)
    forward(3, 1)
    forward(3, 2)
    for kind in (1, 2):
        sent_forward(2, kind)
    start_c(3)
    line_products(3)
    cross_products(3)
    copy_l(2).wait_recv()

    @pl.loop(0, blocks)
    def _(b):
        total = lpair[0, b].astype(f32) + lpair[1, b].astype(f32)
        half = total.astype(bf)
        low_half[b] = half
        extra[block_rows(b), :] = up_factor * lax.dot_general(
            half, uall[owner_of(b)], TN, preferred_element_type=f32
        )

    for p in range(N):
        total = None
        for b in range(p, blocks, N):
            part = lax.dot_general(
                low_half[b],
                g_ref[b * BLOCK : (b + 1) * BLOCK, :],
                NN,
                preferred_element_type=f32,
            )
            total = part if total is None else total + part
        acc[p, :, 0:256] = (total * up_factor).astype(bf)
    for f in range(N):
        esend[f] = acc[position_of(f), :, 0:256]
    for k in range(1, N):
        copy_e(k).start()

    for k in range(1, N):
        copy_e(k).wait_recv()
    grad_up_ref[0] = (esend[z].astype(f32) + erecv[0].astype(f32)) + (
        erecv[1].astype(f32) + erecv[2].astype(f32)
    )
    for k in range(1, N):
        copy_c(k).wait_recv()

    @pl.loop(0, width // COL_STEP)
    def _(i):
        at = pl.ds(pl.multiple_of(i * COL_STEP, COL_STEP), COL_STEP)
        grad_down_ref[0, :, at] = (csend[z, :, at].astype(f32) + crecv[0, :, at].astype(f32)) + (
            crecv[1, :, at].astype(f32) + crecv[2, :, at].astype(f32)
        )

    for h in range(2):
        for k in range(1, N):
            remote(
                psend.at[0, h], prec.at[h, k - 1], send_p.at[0, h], recv_p.at[h, k - 1], owner=mod(own + k)
            ).wait_recv()
        cols = slice(h * HALF, (h + 1) * HALF)

        @pl.loop(0, tokens // ROWS_STEP)
        def _(i):
            at = pl.ds(pl.multiple_of(i * ROWS_STEP, ROWS_STEP), ROWS_STEP)
            total = (own_base[h, at, :] + prec[h, 0, at, :].astype(f32)) + (
                prec[h, 1, at, :].astype(f32) + prec[h, 2, at, :].astype(f32)
            )
            values_ref[at, cols] = total + extra[at, cols]

    for k in range(1, N):
        copy_a(k).wait_send()
        if k < 3:
            copy_b(k).wait_send()
        if k < 3:
            copy_l(k).wait_send()
        copy_c(k).wait_send()
        copy_e(k).wait_send()
    for kind in range(3):
        for way in range(2):
            room = (z > 0) if way == 0 else (z < N - 1)

            @pl.when(room)
            def _():
                copy_z(z, kind, way).wait_send()

        sent_forward(1, kind)
    sent_forward(2, 0)

    for k in range(1, N):
        for c in range(2):
            copy_y(mod(z + k), c).wait_send()
            copy_p(mod(own + k), c).wait_send()


def per_device_fused(
    inputs,
    value_matrix,
    adapter_down_weight,
    adapter_up_weight,
    down_first_moment,
    down_second_moment,
    up_first_moment,
    up_second_moment,
    output_gradient,
    tenant_of_block,
    tenant_storage_slot,
):
    tokens, width = inputs.shape
    blocks = tokens // BLOCK
    bf, f32 = jnp.bfloat16, jnp.float32
    big = jax.ShapeDtypeStruct((1, RANK, width), f32)
    small = jax.ShapeDtypeStruct((1, RANK, 256), f32)
    dma = pltpu.SemaphoreType.DMA
    vmem = pl.BlockSpec(memory_space=pltpu.VMEM)
    smem = pl.BlockSpec(memory_space=pltpu.SMEM)
    hbm = pl.BlockSpec(memory_space=pl.ANY)
    values, grad_down, grad_up = pl.pallas_call(
        fused_kernel,
        out_shape=(
            jax.ShapeDtypeStruct((tokens, 256), f32),
            big,
            small,
        ),
        in_specs=[smem, smem, hbm, vmem, vmem, vmem, hbm],
        out_specs=[vmem] * 3,
        scratch_shapes=[
            pltpu.VMEM((tokens, width), bf),
            pltpu.VMEM((tokens, 256), bf),
            pltpu.VMEM((N, RANK, width), bf),
            pltpu.VMEM((N, 2, CHUNK, width), bf),
            pltpu.VMEM((N, RANK, 256), bf),
            pltpu.VMEM((N, 2, CHUNK, width), bf),
            pltpu.VMEM((N, 2, tokens, HALF), bf),
            pltpu.VMEM((2, 3, tokens, HALF), bf),
            pltpu.VMEM((2, tokens, HALF), f32),
            pltpu.VMEM((2, blocks, RANK, BLOCK), f32),
            pltpu.VMEM((2, blocks, RANK, BLOCK), bf),
            pltpu.VMEM((2, blocks, RANK, BLOCK), f32),
            pltpu.VMEM((2, blocks, RANK, BLOCK), bf),
            pltpu.VMEM((blocks, RANK, BLOCK), bf),
            pltpu.VMEM((blocks, RANK, BLOCK), bf),
            pltpu.VMEM((N, RANK, width), bf),
            pltpu.VMEM((N, RANK, width), bf),
            pltpu.VMEM((N - 1, RANK, width), bf),
            pltpu.VMEM((N, RANK, 256), bf),
            pltpu.VMEM((N - 1, RANK, 256), bf),
            pltpu.VMEM((tokens, 256), f32),
            dma((3,)),
            dma((3,)),
            dma((N, 3, 2)),
            dma((N, 3)),
            dma((N, 2)),
            dma((N, 2)),
            dma((N, 2)),
            dma((2, 3)),
            dma((3,)),
            dma((3,)),
            dma((3,)),
            dma((3,)),
            dma((3,)),
            dma((3,)),
            dma((3,)),
            dma((3,)),
            dma((2,)),
        ],
        compiler_params=pltpu.CompilerParams(
            collective_id=0, has_side_effects=True, vmem_limit_bytes=56 * 1024 * 1024
        ),
    )(
        tenant_of_block,
        tenant_storage_slot,
        inputs,
        value_matrix,
        adapter_down_weight,
        adapter_up_weight,
        output_gradient,
    )
    ndw, ndm, nds = adam_weight_update(
        adapter_down_weight, down_first_moment, down_second_moment, grad_down
    )
    nuw, num, nus = adam_weight_update(
        adapter_up_weight, up_first_moment, up_second_moment, grad_up
    )
    return values.astype(bf), ndw, nuw, ndm, nds, num, nus


def solution(mesh):
    sizes = mesh.shape
    fused = sizes["groups"] == 2 and sizes["fsdp"] == N and sizes["owner"] == N
    in_specs = (
        P(("groups", "fsdp"), "owner"),
        P("fsdp", "owner"),
        P(("groups", "fsdp"), None, "owner"),
        P(("groups", "fsdp"), None, "owner"),
        P(("groups", "fsdp"), None, "owner"),
        P(("groups", "fsdp"), None, "owner"),
        P(("groups", "fsdp"), None, "owner"),
        P(("groups", "fsdp"), None, "owner"),
        P(("groups", "fsdp"), "owner"),
        P("groups"),
        P("groups"),
    )
    out_specs = (
        P(("groups", "fsdp"), "owner"),
        P(("groups", "fsdp"), None, "owner"),
        P(("groups", "fsdp"), None, "owner"),
        P(("groups", "fsdp"), None, "owner"),
        P(("groups", "fsdp"), None, "owner"),
        P(("groups", "fsdp"), None, "owner"),
        P(("groups", "fsdp"), None, "owner"),
    )
    return jax.shard_map(
        per_device_fused if fused else per_device, mesh=mesh, in_specs=in_specs, out_specs=out_specs, check_vma=False
    )
```
